512 devices in a mesh: tile: 32 (over z, core), tp: 16 (over y, x).
Axes of the slice: x: 4, y: 4, z: 16, core: 2. Of those that a mesh axis runs over, the one named last changes fastest.
Arguments:
- tokens: bfloat16 [16384, 1280], P('tile', 'tp'), may hold values from -6 to 6
- mask: int32 [32, 512], P('tile'), may hold values from 0 to 1, as said below
- ln1_gain: float32 [1280], replicated, may hold values from 0.1 to 1.9
- w_query: bfloat16 [1280, 1280], P(None, 'tp'), may hold values from -0.15625 to 0.15625
- w_key: bfloat16 [1280, 1280], P(None, 'tp'), may hold values from -0.15625 to 0.15625
- w_value: bfloat16 [1280, 1280], P(None, 'tp'), may hold values from -0.15625 to 0.15625
- w_out: bfloat16 [1280, 1280], P('tp'), may hold values from -0.15625 to 0.15625
- ln2_gain: float32 [1280], replicated, may hold values from 0.1 to 1.9
- w_in: bfloat16 [1280, 5120], P(None, 'tp'), may hold values from -0.15625 to 0.15625
- w_back: bfloat16 [5120, 1280], P('tp'), may hold values from -0.078125 to 0.078125
Outputs:
- encoded: bfloat16 [16384, 1280], P('tile', 'tp')
The draws below stay inside these ranges and needn't reach their ends.
Inputs may be any that keep to these rules, and one draw needn't show every extreme that they name: `mask`: tile t has between 128 and 384 visible tokens, tile 0 exactly 384, and the visible counts of tiles t and t + 16 add up to 512.
All inputs are finite; a program needn't handle non-finite values.
Results may differ from the reference program's by a relative error of at most 0.009.
Values may be sent and summed in bfloat16 or wider, within the bound.
A program may use at most 64 MiB of HBM per device.

```python
import jax
import jax.numpy as jnp
from jax import lax

D = 1280
FF = 5120
HEADS = 16
P_SIZE = 512
HEAD_DIM = 80
TILES = 32


def draw_mask(key, part):
    key = jax.random.fold_in(key, 11)
    key_counts, key_ranks = jax.random.split(key)
    half_tiles = TILES // 2
    lower = jax.random.randint(key_counts, (half_tiles,), P_SIZE // 4, 3 * P_SIZE // 4 + 1)
    lower = lower.at[0].set(3 * P_SIZE // 4)
    counts = jnp.concatenate([lower, P_SIZE - lower]).astype(jnp.int32)
    ranks = jax.vmap(lambda k: jax.random.permutation(k, P_SIZE))(jax.random.split(key_ranks, TILES))
    return (ranks < counts[:, None]).astype(jnp.int32)


def levels(key, dims, pieces, smallest, high):
    def one(position, shards_of):
        steps = jax.random.uniform(jax.random.fold_in(jax.random.fold_in(key, 6), position), (shards_of,), jnp.float32, smallest / len(pieces), high / len(pieces))
        return jnp.repeat(jnp.exp(steps), dims[position] // shards_of).reshape((-1,) + (1,) * (len(dims) - position - 1))

    level = one(*pieces[0])
    for cut in pieces[1:]:
        level = level * one(*cut)
    return level


def normal_values(rng, shape, width, limit, cuts=(), held_as=jnp.bfloat16):
    array = width * jax.random.normal(rng, shape, jnp.float32)
    if cuts:
        array = array * levels(rng, shape, cuts, -0.22, 0.18)
    return jnp.clip(array, -limit, limit).astype(held_as)


def setup_inputs(seed: int = 0) -> dict:
    splits = jax.random.split(jax.random.key(seed), 11)
    return {
        "tokens": normal_values(splits[0], (TILES * P_SIZE, D), 1.0, 6.0, ((0, 32), (1, 16))),
        "mask": draw_mask(jax.random.fold_in(splits[10], 71), 0),
        "ln1_gain": jnp.clip(1.0 + 0.18 * jax.random.normal(splits[2], (D,), jnp.float32), 0.1, 1.9),
        "w_query": normal_values(splits[3], (D, D), D ** -0.5, 0.15625, ((1, 16),)),
        "w_key": normal_values(splits[4], (D, D), D ** -0.5, 0.15625, ((1, 16),)),
        "w_value": normal_values(splits[5], (D, D), D ** -0.5, 0.15625, ((1, 16),)),
        "w_out": normal_values(splits[6], (D, D), D ** -0.5, 0.15625, ((0, 16),)),
        "ln2_gain": jnp.clip(1.0 + 0.18 * jax.random.normal(splits[7], (D,), jnp.float32), 0.1, 1.9),
        "w_in": normal_values(splits[8], (D, FF), D ** -0.5, 0.15625, ((1, 16),)),
        "w_back": normal_values(splits[9], (FF, D), FF ** -0.5, 0.078125, ((0, 16),)),
    }


def normalize(rows, gain):
    rows = rows.astype(jnp.float32)
    mean = lax.optimization_barrier(jnp.mean(rows, axis=-1, keepdims=True))
    centred = rows - mean
    var = lax.optimization_barrier(jnp.mean(centred * centred, axis=-1, keepdims=True))
    return centred * lax.rsqrt(var + 1e-06) * gain

def reference(tokens, mask, ln1_gain, w_query, w_key, w_value, w_out, ln2_gain, w_in, w_back):
    a_one = normalize(tokens, ln1_gain).astype(jnp.bfloat16)
    query = jnp.dot(a_one, w_query, preferred_element_type=jnp.float32).astype(jnp.bfloat16)
    keys = jnp.dot(a_one, w_key, preferred_element_type=jnp.float32).astype(jnp.bfloat16)
    values = jnp.dot(a_one, w_value, preferred_element_type=jnp.float32).astype(jnp.bfloat16)
    query = query.reshape(TILES, P_SIZE, HEADS, HEAD_DIM)
    zero_tile = jnp.zeros((1, P_SIZE, HEADS, HEAD_DIM), jnp.bfloat16)
    keys_pad = jnp.concatenate([zero_tile, keys.reshape(TILES, P_SIZE, HEADS, HEAD_DIM), zero_tile], 0)
    values_pad = jnp.concatenate([zero_tile, values.reshape(TILES, P_SIZE, HEADS, HEAD_DIM), zero_tile], 0)
    zero_flags = jnp.zeros((1, P_SIZE), jnp.int32)
    flags_pad = jnp.concatenate([zero_flags, mask, zero_flags], 0)

    def one_tile(index):
        index = index.astype(jnp.int32)
        near_keys = lax.dynamic_slice_in_dim(keys_pad, index, 3, 0).reshape(3 * P_SIZE, HEADS, HEAD_DIM)
        near_values = lax.dynamic_slice_in_dim(values_pad, index, 3, 0).reshape(3 * P_SIZE, HEADS, HEAD_DIM)
        near_flags = lax.dynamic_slice_in_dim(flags_pad, index, 3, 0).reshape(3 * P_SIZE)
        own = lax.dynamic_index_in_dim(query, index, 0, keepdims=False)
        scores = jnp.einsum('qhd,khd->hqk', own.astype(jnp.float32), near_keys.astype(jnp.float32))
        scores = scores / jnp.sqrt(jnp.float32(HEAD_DIM))
        scores = jnp.where(near_flags[None, None, :] > 0, scores, jnp.float32(-1e+30))
        probs = jax.nn.softmax(scores, axis=-1).astype(jnp.bfloat16)
        mixed = jnp.einsum('hqk,khd->qhd', probs.astype(jnp.float32), near_values.astype(jnp.float32))
        return mixed.astype(jnp.bfloat16).reshape(P_SIZE, D)
    attended = lax.map(one_tile, jnp.arange(TILES, dtype=jnp.int32)).reshape(TILES * P_SIZE, D)
    hidden = (tokens.astype(jnp.float32) + jnp.dot(attended, w_out, preferred_element_type=jnp.float32)).astype(jnp.bfloat16)
    a_two = normalize(hidden, ln2_gain).astype(jnp.bfloat16)
    inner = jax.nn.gelu(jnp.dot(a_two, w_in, preferred_element_type=jnp.float32)).astype(jnp.bfloat16)
    result = hidden.astype(jnp.float32) + jnp.dot(inner, w_back, preferred_element_type=jnp.float32)
    visible = mask.reshape(TILES * P_SIZE, 1) > 0
    return jnp.where(visible, result, jnp.float32(0.0)).astype(jnp.bfloat16)
```

```python
import functools

import jax
import jax.numpy as jnp
from jax import lax
from jax.experimental import pallas as pl
from jax.experimental.pallas import tpu as pltpu
from jax.sharding import PartitionSpec as P

MESH = pl.DeviceIdType.MESH
D = 1280
FB = 320
HD = 80
SIDE = 4
ROWS = 512
LIVE = 384
CUT = 48
KB = 96
KV = 176
EPS = 1e-06
LOW = -1e30
EXPF = 1.4426950408889634 / (80.0**0.5)
BF = jnp.bfloat16
F32 = jnp.float32


def dot(a, b, dims=((1,), (0,))):
    return lax.dot_general(a, b, (dims, ((), ())), preferred_element_type=F32)


def kernel(
    tok, mask, gain1, gain2, wq, wk, wv, wo, wi, wb, out,
    x1, x2, norm, part, ra, rb, ta, tb, ua, ub, kv, qa, score, prob, place,
    wqkv_t, wo_t, wi_t, wb_t, g1, g2, send, recv,
):
    tp = lax.axis_index("tp")
    tile = lax.axis_index("tile")
    tiles = lax.axis_size("tile")
    xx, yy = lax.rem(tp, SIDE), lax.div(tp, SIDE)

    def xpeer(d):
        return {"tp": yy * SIDE + lax.rem(xx + d, SIDE)}

    def ypeer(d):
        return {"tp": lax.rem(yy + d, SIDE) * SIDE + xx}

    after = {"tile": lax.rem(tile + 1, tiles)}
    before = {"tile": lax.rem(tile + tiles - 1, tiles)}
    peers = [xpeer(d) for d in (1, 2, 3)] + [ypeer(d) for d in (1, 2, 3)] + [after, before]

    barrier = pltpu.get_barrier_semaphore()
    for peer in peers:
        pl.semaphore_signal(barrier, inc=1, device_id=peer, device_id_type=MESH)

    count_sems = [0]

    def push(src, dst, peer):
        k = count_sems[0]
        count_sems[0] += 1
        copy = pltpu.make_async_remote_copy(
            src_ref=src, dst_ref=dst, send_sem=send.at[k], recv_sem=recv.at[k],
            device_id=peer, device_id_type=MESH,
        )
        copy.start()
        return copy

    def finish(copies):
        for copy in copies:
            copy.wait()

    low, high = pl.ds(0, CUT), pl.ds(CUT, HD - CUT)

    flags = mask[...].astype(F32).astype(BF)
    row_i = lax.broadcasted_iota(jnp.int32, (ROWS, ROWS), 0)
    col_i = lax.broadcasted_iota(jnp.int32, (ROWS, ROWS), 1)
    upper = (row_i <= col_i).astype(F32).astype(BF)
    running = dot(jnp.broadcast_to(flags, (16, ROWS)), upper)[0:1, :]
    total = running[0:1, ROWS - 1 : ROWS]
    slot = jnp.where(mask[...] > 0, running - 1.0, -1.0).astype(jnp.int32)
    at = lax.broadcasted_iota(jnp.int32, (LIVE, ROWS), 0) == slot
    place[...] = at.astype(F32).astype(BF)
    tok_t = tok[...].astype(F32).T.astype(BF)
    mine = dot(tok_t, place[...], ((1,), (1,))).astype(BF)
    x1[yy, xx] = mine

    pl.semaphore_wait(barrier, len(peers))

    def gather(buf):
        first = [push(buf.at[yy, xx, low], buf.at[yy, xx, low], xpeer(d)) for d in (1, 2, 3)]
        first += [push(buf.at[yy, xx, high], buf.at[yy, xx, high], ypeer(d)) for d in (1, 2, 3)]
        return first

    def gather_rest(buf, first):
        finish(first)
        rest = [push(buf.at[yy, :, low], buf.at[yy, :, low], ypeer(d)) for d in (1, 2, 3)]
        rest += [push(buf.at[:, xx, high], buf.at[:, xx, high], xpeer(d)) for d in (1, 2, 3)]
        return rest

    first = gather(x1)

    for i, w in enumerate((wq, wk, wv)):
        wqkv_t[HD * i : HD * (i + 1), :] = w[...].astype(F32).T.astype(BF)
    for i in range(D // 128):
        cols = slice(128 * i, 128 * (i + 1))
        g1[cols, :] = jnp.broadcast_to(gain1[:, cols], (128, 128)).T
        g2[cols, :] = jnp.broadcast_to(gain2[:, cols], (128, 128)).T
    rest = gather_rest(x1, first)
    wo_t[...] = wo[...].astype(F32).T.astype(BF)
    for i in range(4):
        wi_t[:, FB * i : FB * (i + 1)] = wi[FB * i : FB * (i + 1), :].astype(F32).T.astype(BF)
        wb_t[FB * i : FB * (i + 1), :] = wb[:, FB * i : FB * (i + 1)].astype(F32).T.astype(BF)
    finish(rest)

    def normalize(buf, gain):
        def shard(i):
            return buf[i // SIDE, i % SIDE].astype(F32)

        total = jnp.zeros((HD, LIVE), F32)
        for i in range(16):
            total += shard(i)
        mean = jnp.sum(total, axis=0, keepdims=True) * (1.0 / D)
        square = jnp.zeros((HD, LIVE), F32)
        for i in range(16):
            centred = shard(i) - mean
            square += centred * centred
        var = jnp.sum(square, axis=0, keepdims=True) * (1.0 / D)
        scale = lax.rsqrt(var + EPS)
        for i in range(16):
            g = gain[HD * i : HD * (i + 1), :]
            g = jnp.concatenate([g, g, g], axis=1)
            norm[HD * i : HD * (i + 1), :] = ((shard(i) - mean) * scale * g).astype(BF)

    normalize(x1, g1)
    qkv = dot(wqkv_t[...], norm[...]).astype(BF)
    valid = lax.broadcasted_iota(jnp.int32, (16, LIVE), 1).astype(F32) < total
    top = lax.broadcasted_iota(jnp.int32, (16, LIVE), 0) == 0
    qa[0:HD, :] = qkv[0:HD]
    qa[HD:KB, :] = top.astype(F32).astype(BF)
    kv[1, 0:HD, :] = qkv[HD : 2 * HD]
    kv[1, HD:KB, :] = jnp.where(valid, 0.0, jnp.where(top, LOW, 0.0)).astype(BF)
    kv[1, KB:KV, :] = qkv[2 * HD :]
    halo = [push(kv.at[1], kv.at[0], after), push(kv.at[1], kv.at[2], before)]
    finish(halo)
    edge = jnp.where(top, LOW, 0.0)
    for i, at_edge in ((0, tile == 0), (2, tile == tiles - 1)):
        off = jnp.where(at_edge, 1.0, 0.0).astype(F32)
        kv[i, HD:KB, :] = (kv[i, HD:KB, :].astype(F32) + edge * off).astype(BF)

    best = jnp.full((8, LIVE), LOW, F32)
    for i in range(3):
        keys = kv[i, 0:KB, :].astype(F32).T.astype(BF)
        s = dot(keys, qa[...])
        score[i] = s
        best = jnp.maximum(best, jnp.max(s.reshape(LIVE // 8, 8, LIVE), axis=0))
    best = jnp.max(best, axis=0, keepdims=True)
    weight = jnp.zeros((8, LIVE), F32)
    mixed = jnp.zeros((HD, LIVE), F32)
    for i in range(3):
        p = jnp.exp2((score[i] - best) * EXPF)
        weight += jnp.sum(p.reshape(LIVE // 8, 8, LIVE), axis=0)
        prob[i] = p.astype(BF)
        mixed += dot(kv[i, KB:KV, :], prob[i])
    weight = jnp.sum(weight, axis=0, keepdims=True)
    o = (mixed / weight).astype(BF)

    def scatter(n):
        first = [push(part.at[n, lax.rem(yy + d, SIDE), :, low], ra.at[n, d - 1], ypeer(d)) for d in (1, 2, 3)]
        first += [push(part.at[n, :, lax.rem(xx + d, SIDE), high], rb.at[n, d - 1], xpeer(d)) for d in (1, 2, 3)]
        finish(first)
        sum_a = part[n, yy, :, low].astype(F32)
        sum_b = part[n, :, xx, high].astype(F32)
        for d in range(3):
            sum_a += ra[n, d].astype(F32)
            sum_b += rb[n, d].astype(F32)
        ta[n] = sum_a.astype(BF)
        tb[n] = sum_b.astype(BF)
        rest = [push(ta.at[n, lax.rem(xx + d, SIDE)], ua.at[n, d - 1], xpeer(d)) for d in (1, 2, 3)]
        rest += [push(tb.at[n, lax.rem(yy + d, SIDE)], ub.at[n, d - 1], ypeer(d)) for d in (1, 2, 3)]
        finish(rest)
        sum_a = ta[n, xx].astype(F32)
        sum_b = tb[n, yy].astype(F32)
        for d in range(3):
            sum_a += ua[n, d].astype(F32)
            sum_b += ub[n, d].astype(F32)
        return jnp.concatenate([sum_a, sum_b], axis=0)

    for i in range(SIDE):
        block = dot(wo_t[FB * i : FB * (i + 1), :], o).astype(BF)
        for j in range(SIDE):
            part[0, i, j] = block[HD * j : HD * (j + 1)]
    hidden = (x1[yy, xx].astype(F32) + scatter(0)).astype(BF)
    x2[yy, xx] = hidden
    finish(gather_rest(x2, gather(x2)))
    normalize(x2, g2)
    inner = jax.nn.gelu(dot(wi_t[...], norm[...])).astype(BF)
    for i in range(SIDE):
        block = dot(wb_t[FB * i : FB * (i + 1), :], inner).astype(BF)
        for j in range(SIDE):
            part[1, i, j] = block[HD * j : HD * (j + 1)]
    done = (x2[yy, xx].astype(F32) + scatter(1)).astype(BF)
    out[...] = dot(done, place[...]).T.astype(BF)


def body(tokens, mask, ln1_gain, w_query, w_key, w_value, w_out, ln2_gain, w_in, w_back):
    v = pl.BlockSpec(memory_space=pltpu.VMEM)
    n_sem = 64
    return pl.pallas_call(
        kernel,
        out_shape=jax.ShapeDtypeStruct(tokens.shape, tokens.dtype),
        in_specs=[v] * 10,
        out_specs=v,
        scratch_shapes=[
            pltpu.VMEM((SIDE, SIDE, HD, LIVE), BF),
            pltpu.VMEM((SIDE, SIDE, HD, LIVE), BF),
            pltpu.VMEM((D, LIVE), BF),
            pltpu.VMEM((2, SIDE, SIDE, HD, LIVE), BF),
            pltpu.VMEM((2, 3, SIDE, CUT, LIVE), BF),
            pltpu.VMEM((2, 3, SIDE, HD - CUT, LIVE), BF),
            pltpu.VMEM((2, SIDE, CUT, LIVE), BF),
            pltpu.VMEM((2, SIDE, HD - CUT, LIVE), BF),
            pltpu.VMEM((2, 3, CUT, LIVE), BF),
            pltpu.VMEM((2, 3, HD - CUT, LIVE), BF),
            pltpu.VMEM((3, KV, LIVE), BF),
            pltpu.VMEM((KB, LIVE), BF),
            pltpu.VMEM((3, LIVE, LIVE), F32),
            pltpu.VMEM((3, LIVE, LIVE), BF),
            pltpu.VMEM((LIVE, ROWS), BF),
            pltpu.VMEM((3 * HD, D), BF),
            pltpu.VMEM((D, HD), BF),
            pltpu.VMEM((FB, D), BF),
            pltpu.VMEM((D, FB), BF),
            pltpu.VMEM((D, 128), F32),
            pltpu.VMEM((D, 128), F32),
            pltpu.SemaphoreType.DMA((n_sem,)),
            pltpu.SemaphoreType.DMA((n_sem,)),
        ],
        compiler_params=pltpu.CompilerParams(
            collective_id=0, has_side_effects=True, vmem_limit_bytes=52 * 2**20
        ),
    )(tokens, mask, ln1_gain.reshape(1, D), ln2_gain.reshape(1, D), w_query, w_key, w_value, w_out, w_in, w_back)


def solution(mesh):
    placed = (
        P("tile", "tp"),
        P("tile", None),
        P(),
        P(None, "tp"),
        P(None, "tp"),
        P(None, "tp"),
        P("tp", None),
        P(),
        P(None, "tp"),
        P("tp", None),
    )
    return jax.shard_map(
        body, mesh=mesh, in_specs=placed, out_specs=P("tile", "tp"), check_vma=False
    )
```

```python
import functools

import jax
import jax.numpy as jnp
from jax import lax
from jax.experimental import pallas as pl
from jax.experimental.pallas import tpu as pltpu
from jax.sharding import PartitionSpec as P

MESH = pl.DeviceIdType.MESH
D = 1280
FB = 320
HD = 80
SIDE = 4
ROWS = 512
LIVE = 384
CUT = 48
KB = 96
KV = 176
EPS = 1e-06
LOW = -1e30
EXPF = 1.4426950408889634 / (80.0**0.5)
BF = jnp.bfloat16
F32 = jnp.float32


def dot(a, b, dims=((1,), (0,))):
    return lax.dot_general(a, b, (dims, ((), ())), preferred_element_type=F32)


def kernel(
    tok_h, mask_h, gain1_h, gain2_h, wq, wk, wv, wo, wi, wb, out,
    tok, mask, gain1, gain2,
    x1, x2, norm, part, ra, rb, ta, tb, ua, ub, kv, qa, score, prob, place,
    wqkv_t, wo_v, wi_t, wb_v, wo_t, wb_t, g1, g2, send, recv, load,
):
    loads = [
        pltpu.make_async_copy(w, v, load.at[i])
        for i, (w, v) in enumerate(
            (
                (mask_h, mask),
                (tok_h, tok),
                (gain1_h, gain1),
                (gain2_h, gain2),
                (wq, wqkv_t.at[pl.ds(0, HD)]),
                (wk, wqkv_t.at[pl.ds(HD, HD)]),
                (wv, wqkv_t.at[pl.ds(2 * HD, HD)]),
                (wo, wo_v),
                (wi, wi_t),
                (wb, wb_v),
            )
        )
    ]
    for copy in loads:
        copy.start()
    tp = lax.axis_index("tp")
    tile = lax.axis_index("tile")
    tiles = lax.axis_size("tile")
    xx, yy = lax.rem(tp, SIDE), lax.div(tp, SIDE)

    def xpeer(d):
        return {"tp": yy * SIDE + lax.rem(xx + d, SIDE)}

    def ypeer(d):
        return {"tp": lax.rem(yy + d, SIDE) * SIDE + xx}

    after = {"tile": lax.rem(tile + 1, tiles)}
    before = {"tile": lax.rem(tile + tiles - 1, tiles)}
    peers = [xpeer(d) for d in (1, 2, 3)] + [ypeer(d) for d in (1, 2, 3)] + [after, before]

    barrier = pltpu.get_barrier_semaphore()
    for peer in peers:
        pl.semaphore_signal(barrier, inc=1, device_id=peer, device_id_type=MESH)

    count_sems = [0]

    def push(src, dst, peer):
        k = count_sems[0]
        count_sems[0] += 1
        copy = pltpu.make_async_remote_copy(
            src_ref=src, dst_ref=dst, send_sem=send.at[k], recv_sem=recv.at[k],
            device_id=peer, device_id_type=MESH,
        )
        copy.start()
        return copy

    def finish(copies):
        for copy in copies:
            copy.wait()

    low, high = pl.ds(0, CUT), pl.ds(CUT, HD - CUT)

    loads[0].wait()
    flags = mask[...].astype(F32).astype(BF)
    row_i = lax.broadcasted_iota(jnp.int32, (ROWS, ROWS), 0)
    col_i = lax.broadcasted_iota(jnp.int32, (ROWS, ROWS), 1)
    upper = (row_i <= col_i).astype(F32).astype(BF)
    running = dot(jnp.broadcast_to(flags, (16, ROWS)), upper)[0:1, :]
    total = running[0:1, ROWS - 1 : ROWS]
    slot = jnp.where(mask[...] > 0, running - 1.0, -1.0).astype(jnp.int32)
    at = lax.broadcasted_iota(jnp.int32, (LIVE, ROWS), 0) == slot
    place[...] = at.astype(F32).astype(BF)
    loads[1].wait()
    mine = dot(tok[...], place[...], ((1,), (1,))).astype(BF)
    x1[yy, xx] = mine

    pl.semaphore_wait(barrier, len(peers))

    def gather(buf):
        first = [push(buf.at[yy, xx, low], buf.at[yy, xx, low], xpeer(d)) for d in (1, 2, 3)]
        first += [push(buf.at[yy, xx, high], buf.at[yy, xx, high], ypeer(d)) for d in (1, 2, 3)]
        return first

    def gather_rest(buf, first):
        finish(first)
        rest = [push(buf.at[yy, :, low], buf.at[yy, :, low], ypeer(d)) for d in (1, 2, 3)]
        rest += [push(buf.at[:, xx, high], buf.at[:, xx, high], xpeer(d)) for d in (1, 2, 3)]
        return rest

    first = gather(x1)

    for copy in loads[2:]:
        copy.wait()
    for i in range(D // 128):
        cols = slice(128 * i, 128 * (i + 1))
        g1[cols, :] = jnp.broadcast_to(gain1[cols].reshape(1, 128), (128, 128)).T
        g2[cols, :] = jnp.broadcast_to(gain2[cols].reshape(1, 128), (128, 128)).T
    rest = gather_rest(x1, first)
    wo_t[...] = wo_v[...].T
    for i in range(4):
        wb_t[FB * i : FB * (i + 1), :] = wb_v[:, FB * i : FB * (i + 1)].T
    finish(rest)

    def normalize(buf, gain):
        def shard(i):
            return buf[i // SIDE, i % SIDE].astype(F32)

        total = jnp.zeros((HD, LIVE), F32)
        for i in range(16):
            total += shard(i)
        mean = jnp.sum(total, axis=0, keepdims=True) * (1.0 / D)
        square = jnp.zeros((HD, LIVE), F32)
        for i in range(16):
            centred = shard(i) - mean
            square += centred * centred
        var = jnp.sum(square, axis=0, keepdims=True) * (1.0 / D)
        scale = lax.rsqrt(var + EPS)
        for i in range(16):
            g = gain[HD * i : HD * (i + 1), :]
            g = jnp.concatenate([g, g, g], axis=1)
            norm[HD * i : HD * (i + 1), :] = ((shard(i) - mean) * scale * g).astype(BF)

    normalize(x1, g1)
    qkv = dot(wqkv_t[...], norm[...]).astype(BF)
    valid = lax.broadcasted_iota(jnp.int32, (16, LIVE), 1).astype(F32) < total
    top = lax.broadcasted_iota(jnp.int32, (16, LIVE), 0) == 0
    qa[0:HD, :] = qkv[0:HD]
    qa[HD:KB, :] = top.astype(F32).astype(BF)
    kv[1, 0:HD, :] = qkv[HD : 2 * HD]
    kv[1, HD:KB, :] = jnp.where(valid, 0.0, jnp.where(top, LOW, 0.0)).astype(BF)
    kv[1, KB:KV, :] = qkv[2 * HD :]
    halo = [push(kv.at[1], kv.at[0], after), push(kv.at[1], kv.at[2], before)]
    finish(halo)
    edge = jnp.where(top, LOW, 0.0)
    for i, at_edge in ((0, tile == 0), (2, tile == tiles - 1)):
        off = jnp.where(at_edge, 1.0, 0.0).astype(F32)
        kv[i, HD:KB, :] = (kv[i, HD:KB, :].astype(F32) + edge * off).astype(BF)

    best = jnp.full((8, LIVE), LOW, F32)
    for i in range(3):
        keys = kv[i, 0:KB, :].astype(F32).T.astype(BF)
        s = dot(keys, qa[...])
        score[i] = s
        best = jnp.maximum(best, jnp.max(s.reshape(LIVE // 8, 8, LIVE), axis=0))
    best = jnp.max(best, axis=0, keepdims=True)
    weight = jnp.zeros((8, LIVE), F32)
    mixed = jnp.zeros((HD, LIVE), F32)
    for i in range(3):
        p = jnp.exp2((score[i] - best) * EXPF)
        weight += jnp.sum(p.reshape(LIVE // 8, 8, LIVE), axis=0)
        prob[i] = p.astype(BF)
        mixed += dot(kv[i, KB:KV, :], prob[i])
    weight = jnp.sum(weight, axis=0, keepdims=True)
    o = (mixed / weight).astype(BF)

    def scatter(n):
        first = [push(part.at[n, lax.rem(yy + d, SIDE), :, low], ra.at[n, d - 1], ypeer(d)) for d in (1, 2, 3)]
        first += [push(part.at[n, :, lax.rem(xx + d, SIDE), high], rb.at[n, d - 1], xpeer(d)) for d in (1, 2, 3)]
        finish(first)
        sum_a = part[n, yy, :, low].astype(F32)
        sum_b = part[n, :, xx, high].astype(F32)
        for d in range(3):
            sum_a += ra[n, d].astype(F32)
            sum_b += rb[n, d].astype(F32)
        ta[n] = sum_a.astype(BF)
        tb[n] = sum_b.astype(BF)
        rest = [push(ta.at[n, lax.rem(xx + d, SIDE)], ua.at[n, d - 1], xpeer(d)) for d in (1, 2, 3)]
        rest += [push(tb.at[n, lax.rem(yy + d, SIDE)], ub.at[n, d - 1], ypeer(d)) for d in (1, 2, 3)]
        finish(rest)
        sum_a = ta[n, xx].astype(F32)
        sum_b = tb[n, yy].astype(F32)
        for d in range(3):
            sum_a += ua[n, d].astype(F32)
            sum_b += ub[n, d].astype(F32)
        return jnp.concatenate([sum_a, sum_b], axis=0)

    for i in range(SIDE):
        block = dot(wo_t[FB * i : FB * (i + 1), :], o).astype(BF)
        for j in range(SIDE):
            part[0, i, j] = block[HD * j : HD * (j + 1)]
    hidden = (x1[yy, xx].astype(F32) + scatter(0)).astype(BF)
    x2[yy, xx] = hidden
    finish(gather_rest(x2, gather(x2)))
    normalize(x2, g2)
    inner = jax.nn.gelu(dot(wi_t[...], norm[...])).astype(BF)
    for i in range(SIDE):
        block = dot(wb_t[FB * i : FB * (i + 1), :], inner).astype(BF)
        for j in range(SIDE):
            part[1, i, j] = block[HD * j : HD * (j + 1)]
    done = (x2[yy, xx].astype(F32) + scatter(1)).astype(BF)
    out[...] = dot(done, place[...]).astype(BF)


def body(tokens, mask, ln1_gain, w_query, w_key, w_value, w_out, ln2_gain, w_in, w_back):
    h = pl.BlockSpec(memory_space=pltpu.HBM)
    n_sem = 64
    return pl.pallas_call(
        kernel,
        out_shape=jax.ShapeDtypeStruct((HD, ROWS), tokens.dtype),
        in_specs=[h] * 10,
        out_specs=pl.BlockSpec(memory_space=pltpu.VMEM),
        scratch_shapes=[
            pltpu.VMEM((HD, ROWS), BF),
            pltpu.VMEM((1, ROWS), jnp.int32),
            pltpu.VMEM((D,), F32),
            pltpu.VMEM((D,), F32),
            pltpu.VMEM((SIDE, SIDE, HD, LIVE), BF),
            pltpu.VMEM((SIDE, SIDE, HD, LIVE), BF),
            pltpu.VMEM((D, LIVE), BF),
            pltpu.VMEM((2, SIDE, SIDE, HD, LIVE), BF),
            pltpu.VMEM((2, 3, SIDE, CUT, LIVE), BF),
            pltpu.VMEM((2, 3, SIDE, HD - CUT, LIVE), BF),
            pltpu.VMEM((2, SIDE, CUT, LIVE), BF),
            pltpu.VMEM((2, SIDE, HD - CUT, LIVE), BF),
            pltpu.VMEM((2, 3, CUT, LIVE), BF),
            pltpu.VMEM((2, 3, HD - CUT, LIVE), BF),
            pltpu.VMEM((3, KV, LIVE), BF),
            pltpu.VMEM((KB, LIVE), BF),
            pltpu.VMEM((3, LIVE, LIVE), F32),
            pltpu.VMEM((3, LIVE, LIVE), BF),
            pltpu.VMEM((LIVE, ROWS), BF),
            pltpu.VMEM((3 * HD, D), BF),
            pltpu.VMEM((HD, D), BF),
            pltpu.VMEM((FB, D), BF),
            pltpu.VMEM((FB, D), BF),
            pltpu.VMEM((D, HD), BF),
            pltpu.VMEM((D, FB), BF),
            pltpu.VMEM((D, 128), F32),
            pltpu.VMEM((D, 128), F32),
            pltpu.SemaphoreType.DMA((n_sem,)),
            pltpu.SemaphoreType.DMA((n_sem,)),
            pltpu.SemaphoreType.DMA((10,)),
        ],
        compiler_params=pltpu.CompilerParams(
            collective_id=0, has_side_effects=True, vmem_limit_bytes=60 * 2**20
        ),
    )(tokens.T, mask, ln1_gain, ln2_gain, w_query.T, w_key.T, w_value.T, w_out, w_in.T, w_back).T


def solution(mesh):
    placed = (
        P("tile", "tp"),
        P("tile", None),
        P(),
        P(None, "tp"),
        P(None, "tp"),
        P(None, "tp"),
        P("tp", None),
        P(),
        P(None, "tp"),
        P("tp", None),
    )
    return jax.shard_map(
        body, mesh=mesh, in_specs=placed, out_specs=P("tile", "tp"), check_vma=False
    )
```

```python
import functools

import jax
import jax.numpy as jnp
from jax import lax
from jax.experimental import pallas as pl
from jax.experimental.pallas import tpu as pltpu
from jax.sharding import PartitionSpec as P

MESH = pl.DeviceIdType.MESH
D = 1280
FB = 320
HD = 80
HALF = 640
SIDE = 4
ROWS = 512
LIVE = 384
CUT = 48
KB = 96
KV = 176
EPS = 1e-06
LOW = -1e30
EXPF = 1.4426950408889634 / (80.0**0.5)
BF = jnp.bfloat16
F32 = jnp.float32


def dot(a, b, dims=((1,), (0,))):
    return lax.dot_general(a, b, (dims, ((), ())), preferred_element_type=F32)


def kernel(
    tok_h, mask_h, gain1_h, gain2_h, wq, wk, wv, wo, wi, wb, out,
    tok, mask, gain1, gain2,
    x1, x2, norm, part, ra, rb, ta, tb, ua, ub, kv, qa, score, prob, place,
    wqkv_t, w, wi_t, wb_v, w_t, wb_t, og, g1, g2, send, recv, load,
):
    tp = lax.axis_index("tp")
    tile = lax.axis_index("tile")
    tiles = lax.axis_size("tile")
    xx, yy = lax.rem(tp, SIDE), lax.div(tp, SIDE)
    core = lax.rem(tile, 2)
    p, q = yy + core * (xx - yy), xx + core * (yy - xx)

    def spot(i):
        y, x = i // SIDE, i % SIDE
        return y + core * (x - y), x + core * (y - x)

    def device(p, q):
        return {"tp": p * (SIDE - 3 * core) + q * (1 + 3 * core)}

    def ppeer(d):
        return device(lax.rem(p + d, SIDE), q)

    def qpeer(d):
        return device(p, lax.rem(q + d, SIDE))

    other = {"tile": tile + 1 - 2 * core}
    loads = [
        pltpu.make_async_copy(w, v, load.at[i])
        for i, (w, v) in enumerate(
            (
                (mask_h, mask),
                (tok_h, tok),
                (gain1_h, gain1),
                (gain2_h, gain2),
                (wq, wqkv_t.at[pl.ds(0, HD)]),
                (wk, wqkv_t.at[pl.ds(HD, HD)]),
                (wv, wqkv_t.at[pl.ds(2 * HD, HD)]),
                (wo.at[:, pl.ds(pl.multiple_of(core * HALF, 128), HALF)], w.at[core, p, q]),
                (wi, wi_t),
                (wb, wb_v),
            )
        )
    ]
    for copy in loads:
        copy.start()

    after = {"tile": lax.rem(tile + 1, tiles)}
    before = {"tile": lax.rem(tile + tiles - 1, tiles)}
    peers = [ppeer(d) for d in (1, 2, 3)] + [qpeer(d) for d in (1, 2, 3)] + [after, before]

    barrier = pltpu.get_barrier_semaphore()
    for peer in peers:
        pl.semaphore_signal(barrier, inc=1, device_id=peer, device_id_type=MESH)

    count_sems = [0]

    def push(src, dst, peer):
        k = count_sems[0]
        count_sems[0] += 1
        copy = pltpu.make_async_remote_copy(
            src_ref=src, dst_ref=dst, send_sem=send.at[k], recv_sem=recv.at[k],
            device_id=peer, device_id_type=MESH,
        )
        copy.start()
        return copy

    def finish(copies):
        for copy in copies:
            copy.wait()

    low, high = pl.ds(0, CUT), pl.ds(CUT, HD - CUT)

    loads[0].wait()
    flags = mask[...].astype(F32).astype(BF)
    row_i = lax.broadcasted_iota(jnp.int32, (ROWS, ROWS), 0)
    col_i = lax.broadcasted_iota(jnp.int32, (ROWS, ROWS), 1)
    upper = (row_i <= col_i).astype(F32).astype(BF)
    running = dot(jnp.broadcast_to(flags, (16, ROWS)), upper)[0:1, :]
    total = running[0:1, ROWS - 1 : ROWS]
    slot = jnp.where(mask[...] > 0, running - 1.0, -1.0).astype(jnp.int32)
    at = lax.broadcasted_iota(jnp.int32, (LIVE, ROWS), 0) == slot
    place[...] = at.astype(F32).astype(BF)
    loads[1].wait()
    mine = dot(tok[...], place[...], ((1,), (1,))).astype(BF)
    x1[p, q] = mine

    pl.semaphore_wait(barrier, len(peers))

    def gather(buf, pre=()):
        def go(part, peer):
            at = buf.at[(*pre, p, q, part)]
            return [push(at, at, peer(d)) for d in (1, 2, 3)]

        return go(low, qpeer) + go(high, ppeer)

    def gather_rest(buf, first, pre=()):
        def go(index, peer):
            at = buf.at[(*pre, *index)]
            return [push(at, at, peer(d)) for d in (1, 2, 3)]

        finish(first)
        return go((p, slice(None), low), ppeer) + go((slice(None), q, high), qpeer)

    first = gather(x1)

    for copy in loads[2:]:
        copy.wait()
    for i in range(D // 128):
        cols = slice(128 * i, 128 * (i + 1))
        g1[cols, :] = jnp.broadcast_to(gain1[cols].reshape(1, 128), (128, 128)).T
        g2[cols, :] = jnp.broadcast_to(gain2[cols].reshape(1, 128), (128, 128)).T
    rest = gather_rest(x1, first)
    w_first = gather(w, (core,))
    for i in range(4):
        wb_t[FB * i : FB * (i + 1), :] = wb_v[:, FB * i : FB * (i + 1)].T
    finish(rest)

    def normalize(buf, gain, where):
        def shard(i):
            return buf[where(i)].astype(F32)

        total = jnp.zeros((HD, LIVE), F32)
        for i in range(16):
            total += shard(i)
        mean = jnp.sum(total, axis=0, keepdims=True) * (1.0 / D)
        square = jnp.zeros((HD, LIVE), F32)
        for i in range(16):
            centred = shard(i) - mean
            square += centred * centred
        var = jnp.sum(square, axis=0, keepdims=True) * (1.0 / D)
        scale = lax.rsqrt(var + EPS)
        for i in range(16):
            g = gain[HD * i : HD * (i + 1), :]
            g = jnp.concatenate([g, g, g], axis=1)
            norm[HD * i : HD * (i + 1), :] = ((shard(i) - mean) * scale * g).astype(BF)

    normalize(x1, g1, spot)
    qkv = dot(wqkv_t[...], norm[...]).astype(BF)
    valid = lax.broadcasted_iota(jnp.int32, (16, LIVE), 1).astype(F32) < total
    top = lax.broadcasted_iota(jnp.int32, (16, LIVE), 0) == 0
    qa[0:HD, :] = qkv[0:HD]
    qa[HD:KB, :] = top.astype(F32).astype(BF)
    kv[1, 0:HD, :] = qkv[HD : 2 * HD]
    kv[1, HD:KB, :] = jnp.where(valid, 0.0, jnp.where(top, LOW, 0.0)).astype(BF)
    kv[1, KB:KV, :] = qkv[2 * HD :]
    halo = [push(kv.at[1], kv.at[0], after), push(kv.at[1], kv.at[2], before)]
    w_rest = gather_rest(w, w_first, (core,))
    finish(halo)
    edge = jnp.where(top, LOW, 0.0)
    for i, at_edge in ((0, tile == 0), (2, tile == tiles - 1)):
        off = jnp.where(at_edge, 1.0, 0.0).astype(F32)
        kv[i, HD:KB, :] = (kv[i, HD:KB, :].astype(F32) + edge * off).astype(BF)

    best = jnp.full((8, LIVE), LOW, F32)
    for i in range(3):
        keys = kv[i, 0:KB, :].astype(F32).T.astype(BF)
        s = dot(keys, qa[...])
        score[i] = s
        best = jnp.maximum(best, jnp.max(s.reshape(LIVE // 8, 8, LIVE), axis=0))
    best = jnp.max(best, axis=0, keepdims=True)
    weight = jnp.zeros((8, LIVE), F32)
    mixed = jnp.zeros((HD, LIVE), F32)
    for i in range(3):
        e = jnp.exp2((score[i] - best) * EXPF)
        weight += jnp.sum(e.reshape(LIVE // 8, 8, LIVE), axis=0)
        prob[i] = e.astype(BF)
        mixed += dot(kv[i, KB:KV, :], prob[i])
    weight = jnp.sum(weight, axis=0, keepdims=True)
    o = (mixed / weight).astype(BF)

    def scatter():
        first = [push(part.at[lax.rem(p + d, SIDE), :, low], ra.at[d - 1], ppeer(d)) for d in (1, 2, 3)]
        first += [push(part.at[:, lax.rem(q + d, SIDE), high], rb.at[d - 1], qpeer(d)) for d in (1, 2, 3)]
        finish(first)
        sum_a = part[p, :, low].astype(F32)
        sum_b = part[:, q, high].astype(F32)
        for d in range(3):
            sum_a += ra[d].astype(F32)
            sum_b += rb[d].astype(F32)
        ta[...] = sum_a.astype(BF)
        tb[...] = sum_b.astype(BF)
        rest = [push(ta.at[lax.rem(q + d, SIDE)], ua.at[d - 1], qpeer(d)) for d in (1, 2, 3)]
        rest += [push(tb.at[lax.rem(p + d, SIDE)], ub.at[d - 1], ppeer(d)) for d in (1, 2, 3)]
        finish(rest)
        sum_a = ta[q].astype(F32)
        sum_b = tb[p].astype(F32)
        for d in range(3):
            sum_a += ua[d].astype(F32)
            sum_b += ub[d].astype(F32)
        return jnp.concatenate([sum_a, sum_b], axis=0)

    og[p, q] = o
    o_first = gather(og)
    finish(w_rest)
    swap = [push(w.at[core, i], w.at[core, :, i], other) for i in range(SIDE)]
    o_rest = gather_rest(og, o_first)

    def turn(half):
        block = w[half].reshape(D, HALF)
        rows = pl.ds(pl.multiple_of(half * HALF, 128), HALF)
        for k in range(D // 128):
            cols = slice(128 * k, 128 * (k + 1))
            w_t[rows, cols] = block[cols].T

    turn(core)
    finish(swap)
    turn(1 - core)
    finish(o_rest)
    o_all = og[...].reshape(D, LIVE)
    for i in range(SIDE):
        block = dot(w_t[FB * i : FB * (i + 1), :], o_all)
        for j in range(SIDE):
            token = x1[spot(SIDE * i + j)].astype(F32)
            x2[i, j] = (token + block[HD * j : HD * (j + 1)]).astype(BF)
    normalize(x2, g2, lambda i: (i // SIDE, i % SIDE))
    inner = jax.nn.gelu(dot(wi_t[...], norm[...])).astype(BF)
    for i in range(SIDE):
        block = dot(wb_t[FB * i : FB * (i + 1), :], inner).astype(BF)
        for j in range(SIDE):
            part[spot(SIDE * i + j)] = block[HD * j : HD * (j + 1)]
    done = (x2[yy, xx].astype(F32) + scatter()).astype(BF)
    out[...] = dot(done, place[...]).astype(BF)


def body(tokens, mask, ln1_gain, w_query, w_key, w_value, w_out, ln2_gain, w_in, w_back):
    h = pl.BlockSpec(memory_space=pltpu.HBM)
    n_sem = 64
    return pl.pallas_call(
        kernel,
        out_shape=jax.ShapeDtypeStruct((HD, ROWS), tokens.dtype),
        in_specs=[h] * 10,
        out_specs=pl.BlockSpec(memory_space=pltpu.VMEM),
        scratch_shapes=[
            pltpu.VMEM((HD, ROWS), BF),
            pltpu.VMEM((1, ROWS), jnp.int32),
            pltpu.VMEM((D,), F32),
            pltpu.VMEM((D,), F32),
            pltpu.VMEM((SIDE, SIDE, HD, LIVE), BF),
            pltpu.VMEM((SIDE, SIDE, HD, LIVE), BF),
            pltpu.VMEM((D, LIVE), BF),
            pltpu.VMEM((SIDE, SIDE, HD, LIVE), BF),
            pltpu.VMEM((3, SIDE, CUT, LIVE), BF),
            pltpu.VMEM((3, SIDE, HD - CUT, LIVE), BF),
            pltpu.VMEM((SIDE, CUT, LIVE), BF),
            pltpu.VMEM((SIDE, HD - CUT, LIVE), BF),
            pltpu.VMEM((3, CUT, LIVE), BF),
            pltpu.VMEM((3, HD - CUT, LIVE), BF),
            pltpu.VMEM((3, KV, LIVE), BF),
            pltpu.VMEM((KB, LIVE), BF),
            pltpu.VMEM((3, LIVE, LIVE), F32),
            pltpu.VMEM((3, LIVE, LIVE), BF),
            pltpu.VMEM((LIVE, ROWS), BF),
            pltpu.VMEM((3 * HD, D), BF),
            pltpu.VMEM((2, SIDE, SIDE, HD, HALF), BF),
            pltpu.VMEM((FB, D), BF),
            pltpu.VMEM((FB, D), BF),
            pltpu.VMEM((D, D), BF),
            pltpu.VMEM((D, FB), BF),
            pltpu.VMEM((SIDE, SIDE, HD, LIVE), BF),
            pltpu.VMEM((D, 128), F32),
            pltpu.VMEM((D, 128), F32),
            pltpu.SemaphoreType.DMA((n_sem,)),
            pltpu.SemaphoreType.DMA((n_sem,)),
            pltpu.SemaphoreType.DMA((10,)),
        ],
        compiler_params=pltpu.CompilerParams(
            collective_id=0, has_side_effects=True, vmem_limit_bytes=60 * 2**20
        ),
    )(tokens.T, mask, ln1_gain, ln2_gain, w_query.T, w_key.T, w_value.T, w_out, w_in.T, w_back).T


def solution(mesh):
    placed = (
        P("tile", "tp"),
        P("tile", None),
        P(),
        P(None, "tp"),
        P(None, "tp"),
        P(None, "tp"),
        P("tp", None),
        P(),
        P(None, "tp"),
        P("tp", None),
    )
    return jax.shard_map(
        body, mesh=mesh, in_specs=placed, out_specs=P("tile", "tp"), check_vma=False
    )
```

```python
import functools

import jax
import jax.numpy as jnp
from jax import lax
from jax.experimental import pallas as pl
from jax.experimental.pallas import tpu as pltpu
from jax.sharding import PartitionSpec as P

MESH = pl.DeviceIdType.MESH
D = 1280
FB = 320
HD = 80
HALF = 640
SIDE = 4
ROWS = 512
LIVE = 384
CUT = 48
KB = 96
KV = 176
EPS = 1e-06
LOW = -1e30
EXPF = 1.4426950408889634 / (80.0**0.5)
BF = jnp.bfloat16
F32 = jnp.float32


def dot(a, b, dims=((1,), (0,))):
    return lax.dot_general(a, b, (dims, ((), ())), preferred_element_type=F32)


def kernel(
    tok_h, mask_h, gain1_h, gain2_h, wq, wk, wv, wo, wi, wb, out,
    tok, mask, gain1, gain2,
    x1, x2, norm, part, ra, rb, ta, tb, ua, ub, kv, qa, score, prob, place,
    wqkv_t, w, wi_t, wb_v, w_t, wb_t, og, g1, g2, send, recv, load,
):
    tp = lax.axis_index("tp")
    tile = lax.axis_index("tile")
    tiles = lax.axis_size("tile")
    xx, yy = lax.rem(tp, SIDE), lax.div(tp, SIDE)
    core = lax.rem(tile, 2)
    p, q = yy + core * (xx - yy), xx + core * (yy - xx)

    def spot(i):
        y, x = i // SIDE, i % SIDE
        return y + core * (x - y), x + core * (y - x)

    def device(p, q):
        return {"tp": p * (SIDE - 3 * core) + q * (1 + 3 * core)}

    def ppeer(d):
        return device(lax.rem(p + d, SIDE), q)

    def qpeer(d):
        return device(p, lax.rem(q + d, SIDE))

    other = {"tile": tile + 1 - 2 * core}
    loads = [
        pltpu.make_async_copy(w, v, load.at[i])
        for i, (w, v) in enumerate(
            (
                (mask_h, mask),
                (tok_h, tok),
                (gain1_h, gain1),
                (gain2_h, gain2),
                (wq, wqkv_t.at[pl.ds(0, HD)]),
                (wk, wqkv_t.at[pl.ds(HD, HD)]),
                (wv, wqkv_t.at[pl.ds(2 * HD, HD)]),
                (wo.at[:, pl.ds(pl.multiple_of(core * HALF, 128), HALF)], w.at[core, p, q]),
                (wi, wi_t),
                (wb, wb_v),
            )
        )
    ]
    for copy in loads:
        copy.start()

    after = {"tile": lax.rem(tile + 1, tiles)}
    before = {"tile": lax.rem(tile + tiles - 1, tiles)}
    peers = [ppeer(d) for d in (1, 2, 3)] + [qpeer(d) for d in (1, 2, 3)] + [after, before]

    barrier = pltpu.get_barrier_semaphore()
    for peer in peers:
        pl.semaphore_signal(barrier, inc=1, device_id=peer, device_id_type=MESH)

    count_sems = [0]

    def push(src, dst, peer):
        k = count_sems[0]
        count_sems[0] += 1
        copy = pltpu.make_async_remote_copy(
            src_ref=src, dst_ref=dst, send_sem=send.at[k], recv_sem=recv.at[k],
            device_id=peer, device_id_type=MESH,
        )
        copy.start()
        return copy

    def finish(copies):
        for copy in copies:
            copy.wait()

    low, high = pl.ds(0, CUT), pl.ds(CUT, HD - CUT)

    loads[0].wait()
    flags = mask[...].astype(F32).astype(BF)
    row_i = lax.broadcasted_iota(jnp.int32, (ROWS, ROWS), 0)
    col_i = lax.broadcasted_iota(jnp.int32, (ROWS, ROWS), 1)
    upper = (row_i <= col_i).astype(F32).astype(BF)
    running = dot(jnp.broadcast_to(flags, (16, ROWS)), upper)[0:1, :]
    total = running[0:1, ROWS - 1 : ROWS]
    slot = jnp.where(mask[...] > 0, running - 1.0, -1.0).astype(jnp.int32)
    at = lax.broadcasted_iota(jnp.int32, (LIVE, ROWS), 0) == slot
    place[...] = at.astype(F32).astype(BF)
    loads[1].wait()
    mine = dot(tok[...], place[...], ((1,), (1,))).astype(BF)
    x1[p, q] = mine

    pl.semaphore_wait(barrier, len(peers))

    def gather(buf, pre=()):
        at_low, at_high = buf.at[(*pre, p, q, low)], buf.at[(*pre, p, q, high)]
        near = [push(at_low, at_low, qpeer(d)) for d in (1, 2, 3)]
        near += [push(at_high, at_high, ppeer(d)) for d in (1, 2, 3)]
        own = [push(at_low, at_low, ppeer(d)) for d in (1, 2, 3)]
        own += [push(at_high, at_high, qpeer(d)) for d in (1, 2, 3)]
        return near, own

    def gather_rest(buf, first, pre=()):
        near, rest = first
        for d in (1, 2, 3):
            near[d - 1].wait()
            at = buf.at[(*pre, p, lax.rem(q + SIDE - d, SIDE), low)]
            rest = rest + [push(at, at, ppeer(e)) for e in (1, 2, 3)]
            near[d + 2].wait()
            at = buf.at[(*pre, lax.rem(p + SIDE - d, SIDE), q, high)]
            rest = rest + [push(at, at, qpeer(e)) for e in (1, 2, 3)]
        return rest

    first = gather(x1)

    for copy in loads[2:]:
        copy.wait()
    for i in range(D // 128):
        cols = slice(128 * i, 128 * (i + 1))
        g1[cols, :] = jnp.broadcast_to(gain1[cols].reshape(1, 128), (128, 128)).T
        g2[cols, :] = jnp.broadcast_to(gain2[cols].reshape(1, 128), (128, 128)).T
    rest = gather_rest(x1, first)
    w_first = gather(w, (core,))
    for i in range(4):
        wb_t[FB * i : FB * (i + 1), :] = wb_v[:, FB * i : FB * (i + 1)].T
    finish(rest)

    def normalize(buf, gain, where):
        def shard(i):
            return buf[where(i)].astype(F32)

        total = jnp.zeros((HD, LIVE), F32)
        for i in range(16):
            total += shard(i)
        mean = jnp.sum(total, axis=0, keepdims=True) * (1.0 / D)
        square = jnp.zeros((HD, LIVE), F32)
        for i in range(16):
            centred = shard(i) - mean
            square += centred * centred
        var = jnp.sum(square, axis=0, keepdims=True) * (1.0 / D)
        scale = lax.rsqrt(var + EPS)
        for i in range(16):
            g = gain[HD * i : HD * (i + 1), :]
            g = jnp.concatenate([g, g, g], axis=1)
            norm[HD * i : HD * (i + 1), :] = ((shard(i) - mean) * scale * g).astype(BF)

    normalize(x1, g1, spot)
    qkv = dot(wqkv_t[...], norm[...]).astype(BF)
    valid = lax.broadcasted_iota(jnp.int32, (16, LIVE), 1).astype(F32) < total
    top = lax.broadcasted_iota(jnp.int32, (16, LIVE), 0) == 0
    qa[0:HD, :] = qkv[0:HD]
    qa[HD:KB, :] = top.astype(F32).astype(BF)
    kv[1, 0:HD, :] = qkv[HD : 2 * HD]
    kv[1, HD:KB, :] = jnp.where(valid, 0.0, jnp.where(top, LOW, 0.0)).astype(BF)
    kv[1, KB:KV, :] = qkv[2 * HD :]
    halo = [push(kv.at[1], kv.at[0], after), push(kv.at[1], kv.at[2], before)]
    w_rest = gather_rest(w, w_first, (core,))
    finish(halo)
    edge = jnp.where(top, LOW, 0.0)
    for i, at_edge in ((0, tile == 0), (2, tile == tiles - 1)):
        off = jnp.where(at_edge, 1.0, 0.0).astype(F32)
        kv[i, HD:KB, :] = (kv[i, HD:KB, :].astype(F32) + edge * off).astype(BF)

    best = jnp.full((8, LIVE), LOW, F32)
    for i in range(3):
        keys = kv[i, 0:KB, :].astype(F32).T.astype(BF)
        s = dot(keys, qa[...])
        score[i] = s
        best = jnp.maximum(best, jnp.max(s.reshape(LIVE // 8, 8, LIVE), axis=0))
    best = jnp.max(best, axis=0, keepdims=True)
    weight = jnp.zeros((8, LIVE), F32)
    mixed = jnp.zeros((HD, LIVE), F32)
    for i in range(3):
        e = jnp.exp2((score[i] - best) * EXPF)
        weight += jnp.sum(e.reshape(LIVE // 8, 8, LIVE), axis=0)
        prob[i] = e.astype(BF)
        mixed += dot(kv[i, KB:KV, :], prob[i])
    weight = jnp.sum(weight, axis=0, keepdims=True)
    o = (mixed / weight).astype(BF)

    def scatter():
        first = [push(part.at[lax.rem(p + d, SIDE), :, low], ra.at[d - 1], ppeer(d)) for d in (1, 2, 3)]
        first += [push(part.at[:, lax.rem(q + d, SIDE), high], rb.at[d - 1], qpeer(d)) for d in (1, 2, 3)]
        finish(first)
        sum_a = part[p, :, low].astype(F32)
        sum_b = part[:, q, high].astype(F32)
        for d in range(3):
            sum_a += ra[d].astype(F32)
            sum_b += rb[d].astype(F32)
        ta[...] = sum_a.astype(BF)
        tb[...] = sum_b.astype(BF)
        rest = [push(ta.at[lax.rem(q + d, SIDE)], ua.at[d - 1], qpeer(d)) for d in (1, 2, 3)]
        rest += [push(tb.at[lax.rem(p + d, SIDE)], ub.at[d - 1], ppeer(d)) for d in (1, 2, 3)]
        finish(rest)
        sum_a = ta[q].astype(F32)
        sum_b = tb[p].astype(F32)
        for d in range(3):
            sum_a += ua[d].astype(F32)
            sum_b += ub[d].astype(F32)
        return jnp.concatenate([sum_a, sum_b], axis=0)

    og[p, q] = o
    o_first = gather(og)
    finish(w_rest)
    swap = [push(w.at[core, i], w.at[core, :, i], other) for i in range(SIDE)]
    o_rest = gather_rest(og, o_first)

    def turn(half):
        block = w[half].reshape(D, HALF)
        rows = pl.ds(pl.multiple_of(half * HALF, 128), HALF)
        for k in range(D // 128):
            cols = slice(128 * k, 128 * (k + 1))
            w_t[rows, cols] = block[cols].T

    turn(core)
    finish(swap)
    turn(1 - core)
    finish(o_rest)
    o_all = og[...].reshape(D, LIVE)
    for i in range(SIDE):
        block = dot(w_t[FB * i : FB * (i + 1), :], o_all)
        for j in range(SIDE):
            token = x1[spot(SIDE * i + j)].astype(F32)
            x2[i, j] = (token + block[HD * j : HD * (j + 1)]).astype(BF)
    normalize(x2, g2, lambda i: (i // SIDE, i % SIDE))
    inner = jax.nn.gelu(dot(wi_t[...], norm[...])).astype(BF)
    for i in range(SIDE):
        block = dot(wb_t[FB * i : FB * (i + 1), :], inner).astype(BF)
        for j in range(SIDE):
            part[spot(SIDE * i + j)] = block[HD * j : HD * (j + 1)]
    done = (x2[yy, xx].astype(F32) + scatter()).astype(BF)
    out[...] = dot(done, place[...]).astype(BF)


def body(tokens, mask, ln1_gain, w_query, w_key, w_value, w_out, ln2_gain, w_in, w_back):
    h = pl.BlockSpec(memory_space=pltpu.HBM)
    n_sem = 112
    return pl.pallas_call(
        kernel,
        out_shape=jax.ShapeDtypeStruct((HD, ROWS), tokens.dtype),
        in_specs=[h] * 10,
        out_specs=pl.BlockSpec(memory_space=pltpu.VMEM),
        scratch_shapes=[
            pltpu.VMEM((HD, ROWS), BF),
            pltpu.VMEM((1, ROWS), jnp.int32),
            pltpu.VMEM((D,), F32),
            pltpu.VMEM((D,), F32),
            pltpu.VMEM((SIDE, SIDE, HD, LIVE), BF),
            pltpu.VMEM((SIDE, SIDE, HD, LIVE), BF),
            pltpu.VMEM((D, LIVE), BF),
            pltpu.VMEM((SIDE, SIDE, HD, LIVE), BF),
            pltpu.VMEM((3, SIDE, CUT, LIVE), BF),
            pltpu.VMEM((3, SIDE, HD - CUT, LIVE), BF),
            pltpu.VMEM((SIDE, CUT, LIVE), BF),
            pltpu.VMEM((SIDE, HD - CUT, LIVE), BF),
            pltpu.VMEM((3, CUT, LIVE), BF),
            pltpu.VMEM((3, HD - CUT, LIVE), BF),
            pltpu.VMEM((3, KV, LIVE), BF),
            pltpu.VMEM((KB, LIVE), BF),
            pltpu.VMEM((3, LIVE, LIVE), F32),
            pltpu.VMEM((3, LIVE, LIVE), BF),
            pltpu.VMEM((LIVE, ROWS), BF),
            pltpu.VMEM((3 * HD, D), BF),
            pltpu.VMEM((2, SIDE, SIDE, HD, HALF), BF),
            pltpu.VMEM((FB, D), BF),
            pltpu.VMEM((FB, D), BF),
            pltpu.VMEM((D, D), BF),
            pltpu.VMEM((D, FB), BF),
            pltpu.VMEM((SIDE, SIDE, HD, LIVE), BF),
            pltpu.VMEM((D, 128), F32),
            pltpu.VMEM((D, 128), F32),
            pltpu.SemaphoreType.DMA((n_sem,)),
            pltpu.SemaphoreType.DMA((n_sem,)),
            pltpu.SemaphoreType.DMA((10,)),
        ],
        compiler_params=pltpu.CompilerParams(
            collective_id=0, has_side_effects=True, vmem_limit_bytes=60 * 2**20
        ),
    )(tokens.T, mask, ln1_gain, ln2_gain, w_query.T, w_key.T, w_value.T, w_out, w_in.T, w_back).T


def solution(mesh):
    placed = (
        P("tile", "tp"),
        P("tile", None),
        P(),
        P(None, "tp"),
        P(None, "tp"),
        P(None, "tp"),
        P("tp", None),
        P(),
        P(None, "tp"),
        P("tp", None),
    )
    return jax.shard_map(
        body, mesh=mesh, in_specs=placed, out_specs=P("tile", "tp"), check_vma=False
    )
```

```python
import functools

import jax
import jax.numpy as jnp
from jax import lax
from jax.experimental import pallas as pl
from jax.experimental.pallas import tpu as pltpu
from jax.sharding import PartitionSpec as P

MESH = pl.DeviceIdType.MESH
D = 1280
FB = 320
HD = 80
HALF = 640
SIDE = 4
ROWS = 512
LIVE = 384
CUT = 48
KB = 96
KV = 176
EPS = 1e-06
LOW = -1e30
EXPF = 1.4426950408889634 / (80.0**0.5)
BF = jnp.bfloat16
F32 = jnp.float32


def dot(a, b, dims=((1,), (0,))):
    return lax.dot_general(a, b, (dims, ((), ())), preferred_element_type=F32)


def kernel(
    tok_h, mask_h, gain1_h, gain2_h, wq, wk, wv, wo, wi, wb, out,
    tok, mask, gain1, gain2,
    x1, x2, norm, part, ra, rb, ta, tb, ua, ub, kv, qa, score, prob, place,
    wqkv_t, w, wi_t, wb_v, w_t, wb_t, og, g1, g2, send, recv, load,
):
    tp = lax.axis_index("tp")
    tile = lax.axis_index("tile")
    tiles = lax.axis_size("tile")
    xx, yy = lax.rem(tp, SIDE), lax.div(tp, SIDE)
    core = lax.rem(tile, 2)
    p, q = yy + core * (xx - yy), xx + core * (yy - xx)

    def spot(i):
        y, x = i // SIDE, i % SIDE
        return y + core * (x - y), x + core * (y - x)

    def device(p, q):
        return {"tp": p * (SIDE - 3 * core) + q * (1 + 3 * core)}

    def ppeer(d):
        return device(lax.rem(p + d, SIDE), q)

    def qpeer(d):
        return device(p, lax.rem(q + d, SIDE))

    other = {"tile": tile + 1 - 2 * core}
    loads = [
        pltpu.make_async_copy(w, v, load.at[i])
        for i, (w, v) in enumerate(
            (
                (mask_h, mask),
                (tok_h, tok),
                (gain1_h, gain1),
                (gain2_h, gain2),
                (wq, wqkv_t.at[pl.ds(0, HD)]),
                (wk, wqkv_t.at[pl.ds(HD, HD)]),
                (wv, wqkv_t.at[pl.ds(2 * HD, HD)]),
                (wo.at[:, pl.ds(pl.multiple_of(core * HALF, 128), HALF)], w.at[core, p, q]),
                (wi, wi_t),
                (wb, wb_v),
            )
        )
    ]
    for copy in loads:
        copy.start()

    after = {"tile": lax.rem(tile + 1, tiles)}
    before = {"tile": lax.rem(tile + tiles - 1, tiles)}
    peers = [ppeer(d) for d in (1, 2, 3)] + [qpeer(d) for d in (1, 2, 3)] + [after, before]

    barrier = pltpu.get_barrier_semaphore()
    for peer in peers:
        pl.semaphore_signal(barrier, inc=1, device_id=peer, device_id_type=MESH)

    pushed = []

    def push(src, dst, peer):
        k = len(pushed)
        copy = pltpu.make_async_remote_copy(
            src_ref=src, dst_ref=dst, send_sem=send.at[k], recv_sem=recv.at[k],
            device_id=peer, device_id_type=MESH,
        )
        copy.start()
        pushed.append(copy)
        return copy

    def finish(copies):
        for copy in copies:
            copy.wait_recv()

    low, high = pl.ds(0, CUT), pl.ds(CUT, HD - CUT)

    loads[0].wait()
    flags = mask[...].astype(F32).astype(BF)
    row_i = lax.broadcasted_iota(jnp.int32, (ROWS, ROWS), 0)
    col_i = lax.broadcasted_iota(jnp.int32, (ROWS, ROWS), 1)
    upper = (row_i <= col_i).astype(F32).astype(BF)
    running = dot(jnp.broadcast_to(flags, (16, ROWS)), upper)[0:1, :]
    total = running[0:1, ROWS - 1 : ROWS]
    slot = jnp.where(mask[...] > 0, running - 1.0, -1.0).astype(jnp.int32)
    at = lax.broadcasted_iota(jnp.int32, (LIVE, ROWS), 0) == slot
    place[...] = at.astype(F32).astype(BF)
    loads[1].wait()
    mine = dot(tok[...], place[...], ((1,), (1,))).astype(BF)
    x1[p, q] = mine

    pl.semaphore_wait(barrier, len(peers))

    def gather(buf, pre=()):
        at_low, at_high = buf.at[(*pre, p, q, low)], buf.at[(*pre, p, q, high)]
        near = [push(at_low, at_low, qpeer(d)) for d in (1, 2, 3)]
        near += [push(at_high, at_high, ppeer(d)) for d in (1, 2, 3)]
        own = [push(at_low, at_low, ppeer(d)) for d in (1, 2, 3)]
        own += [push(at_high, at_high, qpeer(d)) for d in (1, 2, 3)]
        return near, own

    def gather_rest(buf, first, pre=()):
        near, rest = first
        for d in (1, 2, 3):
            near[d - 1].wait_recv()
            at = buf.at[(*pre, p, lax.rem(q + SIDE - d, SIDE), low)]
            rest = rest + [push(at, at, ppeer(e)) for e in (1, 2, 3)]
            near[d + 2].wait_recv()
            at = buf.at[(*pre, lax.rem(p + SIDE - d, SIDE), q, high)]
            rest = rest + [push(at, at, qpeer(e)) for e in (1, 2, 3)]
        return rest

    first = gather(x1)

    for copy in loads[2:]:
        copy.wait()
    for i in range(D // 128):
        cols = slice(128 * i, 128 * (i + 1))
        g1[cols, :] = jnp.broadcast_to(gain1[cols].reshape(1, 128), (128, 128)).T
        g2[cols, :] = jnp.broadcast_to(gain2[cols].reshape(1, 128), (128, 128)).T
    rest = gather_rest(x1, first)
    w_first = gather(w, (core,))
    for i in range(4):
        wb_t[FB * i : FB * (i + 1), :] = wb_v[:, FB * i : FB * (i + 1)].T
    finish(rest)

    def normalize(buf, gain, where):
        def shard(i):
            return buf[where(i)].astype(F32)

        total = jnp.zeros((HD, LIVE), F32)
        for i in range(16):
            total += shard(i)
        mean = jnp.sum(total, axis=0, keepdims=True) * (1.0 / D)
        square = jnp.zeros((HD, LIVE), F32)
        for i in range(16):
            centred = shard(i) - mean
            square += centred * centred
        var = jnp.sum(square, axis=0, keepdims=True) * (1.0 / D)
        scale = lax.rsqrt(var + EPS)
        for i in range(16):
            g = gain[HD * i : HD * (i + 1), :]
            g = jnp.concatenate([g, g, g], axis=1)
            norm[HD * i : HD * (i + 1), :] = ((shard(i) - mean) * scale * g).astype(BF)

    normalize(x1, g1, spot)
    qkv = dot(wqkv_t[...], norm[...]).astype(BF)
    valid = lax.broadcasted_iota(jnp.int32, (16, LIVE), 1).astype(F32) < total
    top = lax.broadcasted_iota(jnp.int32, (16, LIVE), 0) == 0
    qa[0:HD, :] = qkv[0:HD]
    qa[HD:KB, :] = top.astype(F32).astype(BF)
    kv[1, 0:HD, :] = qkv[HD : 2 * HD]
    kv[1, HD:KB, :] = jnp.where(valid, 0.0, jnp.where(top, LOW, 0.0)).astype(BF)
    kv[1, KB:KV, :] = qkv[2 * HD :]
    halo = [push(kv.at[1], kv.at[0], after), push(kv.at[1], kv.at[2], before)]
    w_rest = gather_rest(w, w_first, (core,))
    finish(halo)
    edge = jnp.where(top, LOW, 0.0)
    for i, at_edge in ((0, tile == 0), (2, tile == tiles - 1)):
        off = jnp.where(at_edge, 1.0, 0.0).astype(F32)
        kv[i, HD:KB, :] = (kv[i, HD:KB, :].astype(F32) + edge * off).astype(BF)

    best = jnp.full((8, LIVE), LOW, F32)
    for i in range(3):
        keys = kv[i, 0:KB, :].astype(F32).T.astype(BF)
        s = dot(keys, qa[...])
        score[i] = s
        best = jnp.maximum(best, jnp.max(s.reshape(LIVE // 8, 8, LIVE), axis=0))
    best = jnp.max(best, axis=0, keepdims=True)
    weight = jnp.zeros((8, LIVE), F32)
    mixed = jnp.zeros((HD, LIVE), F32)
    for i in range(3):
        e = jnp.exp2((score[i] - best) * EXPF)
        weight += jnp.sum(e.reshape(LIVE // 8, 8, LIVE), axis=0)
        prob[i] = e.astype(BF)
        mixed += dot(kv[i, KB:KV, :], prob[i])
    weight = jnp.sum(weight, axis=0, keepdims=True)
    o = (mixed / weight).astype(BF)

    def scatter():
        early = list(pushed)
        stage = {}
        for e in (1, 2, 3, 0):
            pe, qe = lax.rem(p + e, SIDE), lax.rem(q + e, SIDE)
            for d in (1, 2, 3):
                pd, qd = lax.rem(p + d, SIDE), lax.rem(q + d, SIDE)
                stage[e, d, 0] = push(part.at[pd, qe, low], ra.at[e, d - 1], ppeer(d))
                stage[e, d, 1] = push(part.at[pe, qd, high], rb.at[e, d - 1], qpeer(d))
        for copy in early:
            copy.wait_send()
        rest = []
        for e in (1, 2, 3, 0):
            sum_a = part[p, lax.rem(q + e, SIDE), low].astype(F32)
            sum_b = part[lax.rem(p + e, SIDE), q, high].astype(F32)
            for d in (1, 2, 3):
                finish([stage[e, d, 0], stage[e, d, 1]])
                sum_a += ra[e, d - 1].astype(F32)
                sum_b += rb[e, d - 1].astype(F32)
            if e:
                ta[e - 1] = sum_a.astype(BF)
                tb[e - 1] = sum_b.astype(BF)
                rest.append(push(ta.at[e - 1], ua.at[e - 1], qpeer(e)))
                rest.append(push(tb.at[e - 1], ub.at[e - 1], ppeer(e)))
        finish(rest)
        for d in range(3):
            sum_a += ua[d].astype(F32)
            sum_b += ub[d].astype(F32)
        for copy in pushed[len(early) :]:
            copy.wait_send()
        return jnp.concatenate([sum_a, sum_b], axis=0)

    og[p, q] = o
    o_first = gather(og)
    finish(w_rest)
    swap = [push(w.at[core, i], w.at[core, :, i], other) for i in range(SIDE)]
    o_rest = gather_rest(og, o_first)

    def turn(half):
        block = w[half].reshape(D, HALF)
        rows = pl.ds(pl.multiple_of(half * HALF, 128), HALF)
        for k in range(D // 128):
            cols = slice(128 * k, 128 * (k + 1))
            w_t[rows, cols] = block[cols].T

    turn(core)
    finish(swap)
    turn(1 - core)
    finish(o_rest)
    o_all = og[...].reshape(D, LIVE)
    for i in range(SIDE):
        block = dot(w_t[FB * i : FB * (i + 1), :], o_all)
        for j in range(SIDE):
            token = x1[spot(SIDE * i + j)].astype(F32)
            x2[i, j] = (token + block[HD * j : HD * (j + 1)]).astype(BF)
    normalize(x2, g2, lambda i: (i // SIDE, i % SIDE))
    inner = jax.nn.gelu(dot(wi_t[...], norm[...])).astype(BF)
    for i in range(SIDE):
        block = dot(wb_t[FB * i : FB * (i + 1), :], inner).astype(BF)
        for j in range(SIDE):
            part[spot(SIDE * i + j)] = block[HD * j : HD * (j + 1)]
    done = (x2[yy, xx].astype(F32) + scatter()).astype(BF)
    out[...] = dot(done, place[...]).astype(BF)


def body(tokens, mask, ln1_gain, w_query, w_key, w_value, w_out, ln2_gain, w_in, w_back):
    h = pl.BlockSpec(memory_space=pltpu.HBM)
    n_sem = 128
    return pl.pallas_call(
        kernel,
        out_shape=jax.ShapeDtypeStruct((HD, ROWS), tokens.dtype),
        in_specs=[h] * 10,
        out_specs=pl.BlockSpec(memory_space=pltpu.VMEM),
        scratch_shapes=[
            pltpu.VMEM((HD, ROWS), BF),
            pltpu.VMEM((1, ROWS), jnp.int32),
            pltpu.VMEM((D,), F32),
            pltpu.VMEM((D,), F32),
            pltpu.VMEM((SIDE, SIDE, HD, LIVE), BF),
            pltpu.VMEM((SIDE, SIDE, HD, LIVE), BF),
            pltpu.VMEM((D, LIVE), BF),
            pltpu.VMEM((SIDE, SIDE, HD, LIVE), BF),
            pltpu.VMEM((SIDE, 3, CUT, LIVE), BF),
            pltpu.VMEM((SIDE, 3, HD - CUT, LIVE), BF),
            pltpu.VMEM((3, CUT, LIVE), BF),
            pltpu.VMEM((3, HD - CUT, LIVE), BF),
            pltpu.VMEM((3, CUT, LIVE), BF),
            pltpu.VMEM((3, HD - CUT, LIVE), BF),
            pltpu.VMEM((3, KV, LIVE), BF),
            pltpu.VMEM((KB, LIVE), BF),
            pltpu.VMEM((3, LIVE, LIVE), F32),
            pltpu.VMEM((3, LIVE, LIVE), BF),
            pltpu.VMEM((LIVE, ROWS), BF),
            pltpu.VMEM((3 * HD, D), BF),
            pltpu.VMEM((2, SIDE, SIDE, HD, HALF), BF),
            pltpu.VMEM((FB, D), BF),
            pltpu.VMEM((FB, D), BF),
            pltpu.VMEM((D, D), BF),
            pltpu.VMEM((D, FB), BF),
            pltpu.VMEM((SIDE, SIDE, HD, LIVE), BF),
            pltpu.VMEM((D, 128), F32),
            pltpu.VMEM((D, 128), F32),
            pltpu.SemaphoreType.DMA((n_sem,)),
            pltpu.SemaphoreType.DMA((n_sem,)),
            pltpu.SemaphoreType.DMA((10,)),
        ],
        compiler_params=pltpu.CompilerParams(
            collective_id=0, has_side_effects=True, vmem_limit_bytes=60 * 2**20
        ),
    )(tokens.T, mask, ln1_gain, ln2_gain, w_query.T, w_key.T, w_value.T, w_out, w_in.T, w_back).T


def solution(mesh):
    placed = (
        P("tile", "tp"),
        P("tile", None),
        P(),
        P(None, "tp"),
        P(None, "tp"),
        P(None, "tp"),
        P("tp", None),
        P(),
        P(None, "tp"),
        P("tp", None),
    )
    return jax.shard_map(
        body, mesh=mesh, in_specs=placed, out_specs=P("tile", "tp"), check_vma=False
    )
```

```python
import functools

import jax
import jax.numpy as jnp
from jax import lax
from jax.experimental import pallas as pl
from jax.experimental.pallas import tpu as pltpu
from jax.sharding import PartitionSpec as P

MESH = pl.DeviceIdType.MESH
D = 1280
FB = 320
HD = 80
HALF = 640
SIDE = 4
ROWS = 512
LIVE = 384
CUT = 48
KB = 96
KV = 176
EPS = 1e-06
LOW = -1e30
EXPF = 1.4426950408889634 / (80.0**0.5)
BF = jnp.bfloat16
F32 = jnp.float32


def dot(a, b, dims=((1,), (0,))):
    return lax.dot_general(a, b, (dims, ((), ())), preferred_element_type=F32)


def kernel(
    tok_h, mask_h, gain1_h, gain2_h, wq, wk, wv, wo, wi, wb, out,
    tok, mask, gain1, gain2,
    x1, x2, norm, part, ra, rb, ta, tb, ua, ub, kv, qa, score, prob, place,
    wqkv_t, w, wi_t, wb_v, w_t, wb_t, og, g1, g2, send, recv, load,
):
    tp = lax.axis_index("tp")
    tile = lax.axis_index("tile")
    tiles = lax.axis_size("tile")
    xx, yy = lax.rem(tp, SIDE), lax.div(tp, SIDE)
    core = lax.rem(tile, 2)
    p, q = yy + core * (xx - yy), xx + core * (yy - xx)

    def spot(i):
        y, x = i // SIDE, i % SIDE
        return y + core * (x - y), x + core * (y - x)

    def device(p, q):
        return {"tp": p * (SIDE - 3 * core) + q * (1 + 3 * core)}

    def ppeer(d):
        return device(lax.rem(p + d, SIDE), q)

    def qpeer(d):
        return device(p, lax.rem(q + d, SIDE))

    other = {"tile": tile + 1 - 2 * core}
    loads = [
        pltpu.make_async_copy(w, v, load.at[i])
        for i, (w, v) in enumerate(
            (
                (mask_h, mask),
                (tok_h, tok),
                (gain1_h, gain1),
                (gain2_h, gain2),
                (wq, wqkv_t.at[pl.ds(0, HD)]),
                (wk, wqkv_t.at[pl.ds(HD, HD)]),
                (wv, wqkv_t.at[pl.ds(2 * HD, HD)]),
                (wo.at[:, pl.ds(pl.multiple_of(core * HALF, 128), HALF)], w.at[core, p, q]),
                (wi, wi_t),
                (wb, wb_v),
            )
        )
    ]
    for copy in loads:
        copy.start()

    after = {"tile": lax.rem(tile + 1, tiles)}
    before = {"tile": lax.rem(tile + tiles - 1, tiles)}
    peers = [ppeer(d) for d in (1, 2, 3)] + [qpeer(d) for d in (1, 2, 3)] + [after, before]

    barrier = pltpu.get_barrier_semaphore()
    for peer in peers:
        pl.semaphore_signal(barrier, inc=1, device_id=peer, device_id_type=MESH)

    pushed = []

    def push(src, dst, peer):
        k = len(pushed)
        copy = pltpu.make_async_remote_copy(
            src_ref=src, dst_ref=dst, send_sem=send.at[k], recv_sem=recv.at[k],
            device_id=peer, device_id_type=MESH,
        )
        copy.start()
        pushed.append(copy)
        return copy

    def finish(copies):
        for copy in copies:
            copy.wait_recv()

    low, high = pl.ds(0, CUT), pl.ds(CUT, HD - CUT)

    loads[0].wait()
    flags = mask[...].astype(F32).astype(BF)
    row_i = lax.broadcasted_iota(jnp.int32, (ROWS, ROWS), 0)
    col_i = lax.broadcasted_iota(jnp.int32, (ROWS, ROWS), 1)
    upper = (row_i <= col_i).astype(F32).astype(BF)
    running = dot(jnp.broadcast_to(flags, (16, ROWS)), upper)[0:1, :]
    total = running[0:1, ROWS - 1 : ROWS]
    slot = jnp.where(mask[...] > 0, running - 1.0, -1.0).astype(jnp.int32)
    at = lax.broadcasted_iota(jnp.int32, (LIVE, ROWS), 0) == slot
    place[...] = at.astype(F32).astype(BF)
    loads[1].wait()
    mine = dot(tok[...], place[...], ((1,), (1,))).astype(BF)
    x1[p, q] = mine

    pl.semaphore_wait(barrier, len(peers))

    def gather(buf, pre=()):
        at_low, at_high = buf.at[(*pre, p, q, low)], buf.at[(*pre, p, q, high)]
        near = [push(at_low, at_low, qpeer(d)) for d in (1, 3, 2)]
        near += [push(at_high, at_high, ppeer(d)) for d in (1, 3, 2)]
        own = [push(at_low, at_low, ppeer(d)) for d in (1, 3, 2)]
        own += [push(at_high, at_high, qpeer(d)) for d in (1, 3, 2)]
        return near, own

    def gather_rest(buf, first, pre=()):
        near, rest = first
        for k, d in enumerate((1, 3, 2)):
            near[k].wait_recv()
            at = buf.at[(*pre, p, lax.rem(q + SIDE - d, SIDE), low)]
            rest = rest + [push(at, at, ppeer(e)) for e in (1, 3, 2)]
            near[k + 3].wait_recv()
            at = buf.at[(*pre, lax.rem(p + SIDE - d, SIDE), q, high)]
            rest = rest + [push(at, at, qpeer(e)) for e in (1, 3, 2)]
        return rest

    first = gather(x1)

    for copy in loads[2:]:
        copy.wait()
    for i in range(D // 128):
        cols = slice(128 * i, 128 * (i + 1))
        g1[cols, :] = jnp.broadcast_to(gain1[cols].reshape(1, 128), (128, 128)).T
        g2[cols, :] = jnp.broadcast_to(gain2[cols].reshape(1, 128), (128, 128)).T
    rest = gather_rest(x1, first)
    w_first = gather(w, (core,))
    for i in range(4):
        wb_t[FB * i : FB * (i + 1), :] = wb_v[:, FB * i : FB * (i + 1)].T
    finish(rest)

    def normalize(buf, gain, where):
        def shard(i):
            return buf[where(i)].astype(F32)

        total = jnp.zeros((HD, LIVE), F32)
        for i in range(16):
            total += shard(i)
        mean = jnp.sum(total, axis=0, keepdims=True) * (1.0 / D)
        square = jnp.zeros((HD, LIVE), F32)
        for i in range(16):
            centred = shard(i) - mean
            square += centred * centred
        var = jnp.sum(square, axis=0, keepdims=True) * (1.0 / D)
        scale = lax.rsqrt(var + EPS)
        for i in range(16):
            g = gain[HD * i : HD * (i + 1), :]
            g = jnp.concatenate([g, g, g], axis=1)
            norm[HD * i : HD * (i + 1), :] = ((shard(i) - mean) * scale * g).astype(BF)

    normalize(x1, g1, spot)
    qkv = dot(wqkv_t[...], norm[...]).astype(BF)
    valid = lax.broadcasted_iota(jnp.int32, (16, LIVE), 1).astype(F32) < total
    top = lax.broadcasted_iota(jnp.int32, (16, LIVE), 0) == 0
    qa[0:HD, :] = qkv[0:HD]
    qa[HD:KB, :] = top.astype(F32).astype(BF)
    kv[1, 0:HD, :] = qkv[HD : 2 * HD]
    kv[1, HD:KB, :] = jnp.where(valid, 0.0, jnp.where(top, LOW, 0.0)).astype(BF)
    kv[1, KB:KV, :] = qkv[2 * HD :]
    halo = [push(kv.at[1], kv.at[0], after), push(kv.at[1], kv.at[2], before)]
    w_rest = gather_rest(w, w_first, (core,))
    best = jnp.full((8, LIVE), LOW, F32)
    for i in (1, 0, 2):
        if i != 1:
            finish([halo[i // 2]])
            edge = jnp.where(top, LOW, 0.0)
            off = jnp.where(tile == (0 if i == 0 else tiles - 1), 1.0, 0.0).astype(F32)
            kv[i, HD:KB, :] = (kv[i, HD:KB, :].astype(F32) + edge * off).astype(BF)
        keys = kv[i, 0:KB, :].astype(F32).T.astype(BF)
        s = dot(keys, qa[...])
        score[i] = s
        best = jnp.maximum(best, jnp.max(s.reshape(LIVE // 8, 8, LIVE), axis=0))
    best = jnp.max(best, axis=0, keepdims=True)
    weight = jnp.zeros((8, LIVE), F32)
    mixed = jnp.zeros((HD, LIVE), F32)
    for i in range(3):
        e = jnp.exp2((score[i] - best) * EXPF)
        weight += jnp.sum(e.reshape(LIVE // 8, 8, LIVE), axis=0)
        prob[i] = e.astype(BF)
        mixed += dot(kv[i, KB:KV, :], prob[i])
    weight = jnp.sum(weight, axis=0, keepdims=True)
    o = (mixed / weight).astype(BF)

    def scatter():
        early = list(pushed)
        first = [push(part.at[lax.rem(p + d, SIDE), :, low], ra.at[d - 1], ppeer(d)) for d in (1, 2, 3)]
        first += [push(part.at[:, lax.rem(q + d, SIDE), high], rb.at[d - 1], qpeer(d)) for d in (1, 2, 3)]
        for copy in early:
            copy.wait_send()
        finish(first)
        sum_a = part[p, :, low].astype(F32)
        sum_b = part[:, q, high].astype(F32)
        for d in range(3):
            sum_a += ra[d].astype(F32)
            sum_b += rb[d].astype(F32)
        ta[...] = sum_a.astype(BF)
        tb[...] = sum_b.astype(BF)
        rest = [push(ta.at[lax.rem(q + d, SIDE)], ua.at[d - 1], qpeer(d)) for d in (1, 2, 3)]
        rest += [push(tb.at[lax.rem(p + d, SIDE)], ub.at[d - 1], ppeer(d)) for d in (1, 2, 3)]
        finish(rest)
        sum_a = ta[q].astype(F32)
        sum_b = tb[p].astype(F32)
        for d in range(3):
            sum_a += ua[d].astype(F32)
            sum_b += ub[d].astype(F32)
        for copy in pushed[len(early) :]:
            copy.wait_send()
        return jnp.concatenate([sum_a, sum_b], axis=0)

    og[p, q] = o
    o_first = gather(og)
    finish(w_rest)
    swap = [push(w.at[core, i], w.at[core, :, i], other) for i in range(SIDE)]
    o_rest = gather_rest(og, o_first)

    def turn(half):
        block = w[half].reshape(D, HALF)
        rows = pl.ds(pl.multiple_of(half * HALF, 128), HALF)
        for k in range(D // 128):
            cols = slice(128 * k, 128 * (k + 1))
            w_t[rows, cols] = block[cols].T

    turn(core)
    finish(swap)
    turn(1 - core)
    finish(o_rest)
    o_all = og[...].reshape(D, LIVE)
    for i in range(SIDE):
        block = dot(w_t[FB * i : FB * (i + 1), :], o_all)
        for j in range(SIDE):
            token = x1[spot(SIDE * i + j)].astype(F32)
            x2[i, j] = (token + block[HD * j : HD * (j + 1)]).astype(BF)
    normalize(x2, g2, lambda i: (i // SIDE, i % SIDE))
    inner = jax.nn.gelu(dot(wi_t[...], norm[...])).astype(BF)
    for i in range(SIDE):
        block = dot(wb_t[FB * i : FB * (i + 1), :], inner).astype(BF)
        for j in range(SIDE):
            part[spot(SIDE * i + j)] = block[HD * j : HD * (j + 1)]
    done = (x2[yy, xx].astype(F32) + scatter()).astype(BF)
    out[...] = dot(done, place[...]).astype(BF)


def body(tokens, mask, ln1_gain, w_query, w_key, w_value, w_out, ln2_gain, w_in, w_back):
    h = pl.BlockSpec(memory_space=pltpu.HBM)
    n_sem = 128
    return pl.pallas_call(
        kernel,
        out_shape=jax.ShapeDtypeStruct((HD, ROWS), tokens.dtype),
        in_specs=[h] * 10,
        out_specs=pl.BlockSpec(memory_space=pltpu.VMEM),
        scratch_shapes=[
            pltpu.VMEM((HD, ROWS), BF),
            pltpu.VMEM((1, ROWS), jnp.int32),
            pltpu.VMEM((D,), F32),
            pltpu.VMEM((D,), F32),
            pltpu.VMEM((SIDE, SIDE, HD, LIVE), BF),
            pltpu.VMEM((SIDE, SIDE, HD, LIVE), BF),
            pltpu.VMEM((D, LIVE), BF),
            pltpu.VMEM((SIDE, SIDE, HD, LIVE), BF),
            pltpu.VMEM((3, SIDE, CUT, LIVE), BF),
            pltpu.VMEM((3, SIDE, HD - CUT, LIVE), BF),
            pltpu.VMEM((SIDE, CUT, LIVE), BF),
            pltpu.VMEM((SIDE, HD - CUT, LIVE), BF),
            pltpu.VMEM((3, CUT, LIVE), BF),
            pltpu.VMEM((3, HD - CUT, LIVE), BF),
            pltpu.VMEM((3, KV, LIVE), BF),
            pltpu.VMEM((KB, LIVE), BF),
            pltpu.VMEM((3, LIVE, LIVE), F32),
            pltpu.VMEM((3, LIVE, LIVE), BF),
            pltpu.VMEM((LIVE, ROWS), BF),
            pltpu.VMEM((3 * HD, D), BF),
            pltpu.VMEM((2, SIDE, SIDE, HD, HALF), BF),
            pltpu.VMEM((FB, D), BF),
            pltpu.VMEM((FB, D), BF),
            pltpu.VMEM((D, D), BF),
            pltpu.VMEM((D, FB), BF),
            pltpu.VMEM((SIDE, SIDE, HD, LIVE), BF),
            pltpu.VMEM((D, 128), F32),
            pltpu.VMEM((D, 128), F32),
            pltpu.SemaphoreType.DMA((n_sem,)),
            pltpu.SemaphoreType.DMA((n_sem,)),
            pltpu.SemaphoreType.DMA((10,)),
        ],
        compiler_params=pltpu.CompilerParams(
            collective_id=0, has_side_effects=True, vmem_limit_bytes=60 * 2**20
        ),
    )(tokens.T, mask, ln1_gain, ln2_gain, w_query.T, w_key.T, w_value.T, w_out, w_in.T, w_back).T


def solution(mesh):
    placed = (
        P("tile", "tp"),
        P("tile", None),
        P(),
        P(None, "tp"),
        P(None, "tp"),
        P(None, "tp"),
        P("tp", None),
        P(),
        P(None, "tp"),
        P("tp", None),
    )
    return jax.shard_map(
        body, mesh=mesh, in_specs=placed, out_specs=P("tile", "tp"), check_vma=False
    )
```
